32 devices in a mesh: group: 4 (over x, core), dp: 2 (over y), tensor: 4 (over z).
Axes of the slice: x: 2, y: 2, z: 4, core: 2. Of those that a mesh axis runs over, the one named last changes fastest.
Arguments:
- keyvalue_local: float32 [4, 2, 4096, 1024], P('group', None, 'dp', 'tensor'), may hold values from -6 to 6
- keyvalue_anchor: float32 [2, 4096, 1024], P(None, 'dp', 'tensor'), may hold values from -6 to 6
- keyvalue_state: float32 [2, 4096, 1024], P(None, 'dp', 'tensor'), may hold values from -6 to 6
- router_local: float32 [4, 4096, 8], P('group', 'dp'), may hold values from -6 to 6
- router_anchor: float32 [4096, 8], P('dp'), may hold values from -6 to 6
- router_state: float32 [4096, 8], P('dp'), may hold values from -6 to 6
- gain_local: float32 [4, 2, 4096], P('group', None, 'dp'), may hold values from -6 to 6
- gain_anchor: float32 [2, 4096], P(None, 'dp'), may hold values from -6 to 6
- gain_state: float32 [2, 4096], P(None, 'dp'), may hold values from -6 to 6
- embed_local: float32 [4, 250, 4096], P('group', 'dp', 'tensor'), may hold values from -6 to 6
- embed_anchor: float32 [250, 4096], P('dp', 'tensor'), may hold values from -6 to 6
- embed_state: float32 [250, 4096], P('dp', 'tensor'), may hold values from -6 to 6
- embed_basis: float32 [4096, 64], P('tensor'), may hold values from -0.25 to 0.25
- outer_rate: float32 [], replicated, may hold values from 0.5 to 1
Outputs:
- keyvalue_average: float32 [2, 4096, 1024], P(None, 'dp', 'tensor')
- keyvalue_momentum: float32 [2, 4096, 1024], P(None, 'dp', 'tensor')
- keyvalue_updated: float32 [2, 4096, 1024], P(None, 'dp', 'tensor')
- router_average: float32 [4096, 8], P('dp')
- router_momentum: float32 [4096, 8], P('dp')
- router_updated: float32 [4096, 8], P('dp')
- gain_average: float32 [2, 4096], P(None, 'dp')
- gain_momentum: float32 [2, 4096], P(None, 'dp')
- gain_updated: float32 [2, 4096], P(None, 'dp')
- embed_average: float32 [250, 4096], P('dp', 'tensor')
- embed_momentum: float32 [250, 4096], P('dp', 'tensor')
- embed_updated: float32 [250, 4096], P('dp', 'tensor')
The draws below stay inside these ranges and needn't reach their ends.
All inputs are finite; a program needn't handle non-finite values.
Results may differ from the reference program's by a relative error of at most 0.0001.
Values sent between devices are 32-bit elements; how exact they have to be, the bound alone decides.
A program may use at most 128 MiB of HBM per device.

```python
import math
import jax
import jax.numpy as jnp
from jax import lax

D = 4096
KV = 1024
EXPERTS = 8
RANK = 64
VOCAB = 250
GROUPS = 4


def level_of(own_key, shape, shards, least, high):
    def one(axis_at, blocks):
        heights = jax.random.uniform(jax.random.fold_in(jax.random.fold_in(own_key, 6), axis_at), (blocks,), jnp.float32, least / len(shards), high / len(shards))
        return jnp.repeat(jnp.exp(heights), shape[axis_at] // blocks).reshape((-1,) + (1,) * (len(shape) - axis_at - 1))

    gain = one(*shards[0])
    for cut in shards[1:]:
        gain = gain * one(*cut)
    return gain


def centred(rng, shape, spread, bound, pieces=(), held_as=jnp.bfloat16):
    values = spread * jax.random.normal(rng, shape, jnp.float32)
    if pieces:
        values = values * level_of(rng, shape, pieces, -0.22, 0.18)
    return jnp.clip(values, -bound, bound).astype(held_as)


def setup_inputs(seed: int = 0) -> dict:
    seeds = jax.random.split(jax.random.key(seed), 15)
    keyvalue_local = centred(seeds[0], (GROUPS, 2, D, KV), 1.0, 6.0, ((0, 4), (2, 2), (3, 4)), jnp.float32)
    keyvalue_anchor = centred(seeds[1], (2, D, KV), 1.0, 6.0, ((1, 2), (2, 4)), jnp.float32)
    keyvalue_state = centred(seeds[2], (2, D, KV), 1.0, 6.0, ((1, 2), (2, 4)), jnp.float32)
    router_local = centred(seeds[3], (GROUPS, D, EXPERTS), 1.0, 6.0, ((0, 4), (1, 2)), jnp.float32)
    router_anchor = centred(seeds[4], (D, EXPERTS), 1.0, 6.0, ((0, 2),), jnp.float32)
    router_state = centred(seeds[5], (D, EXPERTS), 1.0, 6.0, ((0, 2),), jnp.float32)
    gain_local = centred(seeds[6], (GROUPS, 2, D), 1.0, 6.0, ((0, 4), (2, 2)), jnp.float32)
    gain_anchor = centred(seeds[7], (2, D), 1.0, 6.0, ((1, 2),), jnp.float32)
    gain_state = centred(seeds[8], (2, D), 1.0, 6.0, ((1, 2),), jnp.float32)
    embed_local = centred(seeds[9], (GROUPS, VOCAB, D), 1.0, 6.0, ((0, 4), (1, 2), (2, 4)), jnp.float32)
    embed_anchor = centred(seeds[10], (VOCAB, D), 1.0, 6.0, ((0, 2), (1, 4)), jnp.float32)
    embed_state = centred(seeds[11], (VOCAB, D), 1.0, 6.0, ((0, 2), (1, 4)), jnp.float32)
    embed_basis = centred(seeds[12], (D, RANK), (D // 8) ** -0.5, 0.25, ((0, 4),), jnp.float32)
    outer_rate = jnp.clip(jnp.exp(jax.random.uniform(seeds[13], (), jnp.float32, math.log(0.5), math.log(1.0))), 0.5, 1.0)
    return dict(keyvalue_local=keyvalue_local, keyvalue_anchor=keyvalue_anchor, keyvalue_state=keyvalue_state, router_local=router_local, router_anchor=router_anchor, router_state=router_state, gain_local=gain_local, gain_anchor=gain_anchor, gain_state=gain_state, embed_local=embed_local, embed_anchor=embed_anchor, embed_state=embed_state, embed_basis=embed_basis, outer_rate=outer_rate)


def nesterov(average, state, anchor, outer_rate):
    momentum = 0.5 * state + average
    updated = anchor - outer_rate * (average + 0.5 * momentum)
    return average, momentum, updated


def group_mean(anchor, local):
    total = jnp.zeros(anchor.shape, jnp.float32)
    for index in range(GROUPS):
        total = total + (anchor - local[index])
    return total / GROUPS


def reference(keyvalue_local, keyvalue_anchor, keyvalue_state, router_local, router_anchor, router_state, gain_local, gain_anchor, gain_state, embed_local, embed_anchor, embed_state, embed_basis, outer_rate):
    keyvalue_out = nesterov(group_mean(keyvalue_anchor, keyvalue_local), keyvalue_state, keyvalue_anchor, outer_rate)
    router_out = nesterov(group_mean(router_anchor, router_local), router_state, router_anchor, outer_rate)
    gain_out = nesterov(group_mean(gain_anchor, gain_local), gain_state, gain_anchor, outer_rate)
    factors = jnp.zeros((embed_anchor.shape[0], embed_basis.shape[1]), jnp.float32)
    for index in range(GROUPS):
        factors = factors + jnp.dot(embed_anchor - embed_local[index], embed_basis, precision=lax.Precision.HIGHEST, preferred_element_type=jnp.float32)
    factors = factors / GROUPS
    embed_average = jnp.dot(factors, embed_basis.T, precision=lax.Precision.HIGHEST, preferred_element_type=jnp.float32)
    embed_out = nesterov(embed_average, embed_state, embed_anchor, outer_rate)
    return (keyvalue_out[0], keyvalue_out[1], keyvalue_out[2], router_out[0], router_out[1], router_out[2], gain_out[0], gain_out[1], gain_out[2], embed_out[0], embed_out[1], embed_out[2])
```

```python
import functools

import jax
import jax.numpy as jnp
from jax import lax
from jax.experimental import pallas as pl
from jax.experimental.pallas import tpu as pltpu
from jax.sharding import PartitionSpec as P

MESH = pl.DeviceIdType.MESH


def nesterov(average, state, anchor, rate):
    momentum = 0.5 * state + average
    return momentum, anchor - rate * (average + 0.5 * momentum)


def mean(total, groups):
    if groups & (groups - 1) == 0:
        return total * (1.0 / groups)
    return total / float(groups)


def exchange_kernel(
    chips, tensors, chunks, vocab,
    rate_ref, kl, ka, ks, rl, ra, rs, gl, ga, gs, el, ea, es, eb,
    k_avg, k_mom, k_upd, r_avg, r_mom, r_upd, g_avg, g_mom, g_upd, e_avg, e_mom, e_upd,
    a_v, l_v, s_v, pair_v, x_v,
    rl_v, ra_v, rs_v, gl_v, ga_v, gs_v, el_v, ea_v, es_v, eb_v, ed_v,
    r_d, r_pair, r_x, r_a, g_d, g_pair, g_x, g_a, f_d, f_pair, f_x, f_z, f_a,
    a_sem, l_sem, s_sem, small_sem,
    d_send, d_recv, x_send, x_recv, c_send, c_recv,
    sd_send, sd_recv, sx_send, sx_recv, sc_send, sc_recv, z_send, z_recv,
):
    groups = 2 * chips
    me = lax.axis_index("group")
    chip, core = me // 2, lax.rem(me, 2)
    other = 1 - core
    sibling = chip * 2 + other
    lane = lax.axis_index("tensor")
    rows = a_v.shape[1] // chunks
    half_rows = a_v.shape[1]

    def load(src, dst, sem, half, c):
        at = pl.multiple_of(c * rows, rows)
        return pltpu.make_async_copy(
            src.at[half, pl.ds(at, rows), :], dst.at[half, pl.ds(at, rows), :], sem.at[half, c]
        )

    def start_loads(c, _):
        for half in (other, core):
            load(ka, a_v, a_sem, half, c).start()
            load(kl, l_v, l_sem, half, c).start()
        return 0

    small_loads = [
        pltpu.make_async_copy(src, dst, small_sem.at[i])
        for i, (src, dst) in enumerate(
            [(ea, ea_v), (el, el_v), (eb, eb_v), (rl, rl_v), (ra, ra_v), (gl, gl_v), (ga, ga_v),
             (rs, rs_v), (gs, gs_v), (es, es_v)]
        )
    ]
    lead = min(4, chunks)
    lax.fori_loop(0, lead, start_loads, 0)
    for copy in small_loads[:7]:
        copy.start()

    barrier = pltpu.get_barrier_semaphore()
    pl.semaphore_signal(barrier, inc=1, device_id={"group": sibling}, device_id_type=MESH)
    for j in range(1, chips):
        peer = lax.rem(chip + j, chips) * 2 + core
        pl.semaphore_signal(barrier, inc=1, device_id={"group": peer}, device_id_type=MESH)
    for j in range(1, tensors):
        peer = lax.rem(lane + j, tensors)
        pl.semaphore_signal(barrier, inc=1, device_id={"tensor": peer}, device_id_type=MESH)

    lax.fori_loop(lead, chunks, start_loads, 0)
    for copy in small_loads[7:]:
        copy.start()
    s_loads = [
        pltpu.make_async_copy(ks.at[half], s_v.at[half], s_sem.at[half]) for half in (0, 1)
    ]
    for copy in s_loads:
        copy.start()
    pl.semaphore_wait(barrier, chips + tensors - 1)

    def to_sibling(src, dst, send, recv):
        return pltpu.make_async_remote_copy(
            src_ref=src, dst_ref=dst, send_sem=send, recv_sem=recv,
            device_id={"group": sibling}, device_id_type=MESH,
        )

    def to_chip(j, src, dst, send, recv):
        return pltpu.make_async_remote_copy(
            src_ref=src, dst_ref=dst, send_sem=send, recv_sem=recv,
            device_id={"group": lax.rem(chip + j, chips) * 2 + core}, device_id_type=MESH,
        )

    def part(c):
        return pl.ds(pl.multiple_of(c * rows, rows), rows)

    def pair_copy(c):
        return to_sibling(l_v.at[other, part(c), :], pair_v.at[part(c), :], d_send.at[c], d_recv.at[c])

    def chip_copy(c, j, source):
        return to_chip(
            j, x_v.at[source, part(c), :], x_v.at[source, part(c), :],
            x_send.at[j - 1, c], x_recv.at[source, c],
        )

    def share_copy(c, half):
        return to_sibling(k_avg.at[half, part(c), :], k_avg.at[half, part(c), :], c_send.at[c], c_recv.at[c])

    def give(c):
        load(ka, a_v, a_sem, other, c).wait()
        load(kl, l_v, l_sem, other, c).wait()
        l_v[other, part(c), :] = a_v[other, part(c), :] - l_v[other, part(c), :]
        pair_copy(c).start()
        load(ka, a_v, a_sem, core, c).wait()
        load(kl, l_v, l_sem, core, c).wait()

    def send(c):
        copy = pair_copy(c)
        copy.wait_recv()
        x_v[chip, part(c), :] = (
            a_v[core, part(c), :] - l_v[core, part(c), :]
        ) + pair_v[part(c), :]
        for j in range(1, chips):
            chip_copy(c, j, chip).start()

    def give_and_send(c, _):
        give(c)
        send(c - 1)
        return 0

    give(0)
    lax.fori_loop(1, lead, give_and_send, 0)

    for copy in small_loads[:7]:
        copy.wait()
    smalls = [(r_d, r_pair, r_x, r_a), (g_d, g_pair, g_x, g_a), (f_d, f_pair, f_x, f_a)]

    ed_v[...] = jnp.zeros_like(ed_v)
    blocks = el_v.shape[1]
    for b in range(blocks):
        ed_v[0:vocab, b * 128 : (b + 1) * 128] = ea_v[:, b * 128 : (b + 1) * 128] - el_v[:, b, :]
    r_half = r_d.shape[2]
    g_half = g_d.shape[2]
    for h in (0, 1):
        r_d[h] = ra_v[:, h * r_half : (h + 1) * r_half] - rl_v[:, h * r_half : (h + 1) * r_half]
        g_d[h] = ga_v[:, h * g_half : (h + 1) * g_half] - gl_v[:, h * g_half : (h + 1) * g_half]
    factors = lax.dot_general(
        eb_v[...], ed_v[...], (((1,), (1,)), ((), ())),
        precision=lax.Precision.HIGHEST, preferred_element_type=jnp.float32,
    )
    rank_half = f_d.shape[1]
    for h in (0, 1):
        f_d[h] = factors[h * rank_half : (h + 1) * rank_half, :]
    small_pair = [
        to_sibling(d.at[other], pair, sd_send.at[i], sd_recv.at[i])
        for i, (d, pair, x, a) in enumerate(smalls)
    ]
    for copy in small_pair:
        copy.start()
    for i, (d, pair, x, a) in enumerate(smalls):
        small_pair[i].wait_recv()
        x[chip] = d[core] + pair[...]
        for j in range(1, chips):
            to_chip(j, x.at[chip], x.at[chip], sx_send.at[i, j - 1], sx_recv.at[i, chip]).start()

    lax.fori_loop(lead, chunks, give_and_send, 0)
    send(chunks - 1)
    for copy in s_loads + small_loads[7:]:
        copy.wait()

    rate = rate_ref[0]

    def gather(c):
        for j in range(1, chips):
            chip_copy(c, j, lax.rem(chip + j, chips)).wait_recv()
        total = x_v[0, part(c), :]
        for q in range(1, chips):
            total = total + x_v[q, part(c), :]
        average = mean(total, groups)
        k_avg[core, part(c), :] = average
        share_copy(c, core).start()
        momentum, updated = nesterov(average, s_v[core, part(c), :], a_v[core, part(c), :], rate)
        k_mom[core, part(c), :] = momentum
        k_upd[core, part(c), :] = updated

    def accept(c):
        share_copy(c, other).wait_recv()
        momentum, updated = nesterov(
            k_avg[other, part(c), :], s_v[other, part(c), :], a_v[other, part(c), :], rate
        )
        k_mom[other, part(c), :] = momentum
        k_upd[other, part(c), :] = updated

    def gather_and_accept(c, _):
        gather(c)
        accept(c - 1)
        return 0

    cut1 = max(lead, chunks // 2)
    cut2 = max(cut1, (3 * chunks) // 4)
    cut3 = max(cut2, (7 * chunks) // 8)
    gather(0)
    lax.fori_loop(1, cut1, gather_and_accept, 0)

    def small_share(i, half):
        a = smalls[i][3]
        return to_sibling(a.at[half], a.at[half], sc_send.at[i], sc_recv.at[i])

    def z_copy(j, source):
        return pltpu.make_async_remote_copy(
            src_ref=f_z.at[source], dst_ref=f_z.at[source], send_sem=z_send.at[j - 1],
            recv_sem=z_recv.at[source], device_id={"tensor": lax.rem(lane + j, tensors)},
            device_id_type=MESH,
        )

    for i, (d, pair, x, a) in enumerate(smalls):
        for j in range(1, chips):
            q = lax.rem(chip + j, chips)
            to_chip(j, x.at[q], x.at[q], sx_send.at[i, j - 1], sx_recv.at[i, q]).wait_recv()
        total = x[0]
        for q in range(1, chips):
            total = total + x[q]
        if i < 2:
            a[core] = mean(total, groups)
            small_share(i, core).start()
        else:
            f_z[lane] = total
            for j in range(1, tensors):
                z_copy(j, lane).start()

    lax.fori_loop(cut1, cut2, gather_and_accept, 0)

    for j in range(1, tensors):
        z_copy(j, lax.rem(lane + j, tensors)).wait_recv()
    total = f_z[0]
    for t in range(1, tensors):
        total = total + f_z[t]
    f_a[core] = mean(total, groups)
    small_share(2, core).start()
    for i, half, avg, mom, upd, a, st, an in (
        (0, r_half, r_avg, r_mom, r_upd, r_a, rs_v, ra_v),
        (1, g_half, g_avg, g_mom, g_upd, g_a, gs_v, ga_v),
    ):
        small_share(i, other).wait_recv()
        for h in (0, 1):
            at = slice(h * half, (h + 1) * half)
            average = a[h]
            momentum, updated = nesterov(average, st[:, at], an[:, at], rate)
            avg[:, at] = average
            mom[:, at] = momentum
            upd[:, at] = updated

    lax.fori_loop(cut2, cut3, gather_and_accept, 0)

    small_share(2, other).wait_recv()
    turned = jnp.concatenate([f_a[0], f_a[1]], axis=0).T
    average = lax.dot_general(
        turned, eb_v[...], (((1,), (0,)), ((), ())),
        precision=lax.Precision.HIGHEST, preferred_element_type=jnp.float32,
    )[0:vocab, :]
    momentum, updated = nesterov(average, es_v[...], ea_v[...], rate)
    e_avg[...] = average
    e_mom[...] = momentum
    e_upd[...] = updated

    lax.fori_loop(cut3, chunks, gather_and_accept, 0)
    accept(chunks - 1)

    def drain(c, _):
        pair_copy(c).wait_send()
        for j in range(1, chips):
            chip_copy(c, j, chip).wait_send()
        share_copy(c, core).wait_send()
        return 0

    lax.fori_loop(0, chunks, drain, 0)
    for i, (d, pair, x, a) in enumerate(smalls):
        small_pair[i].wait_send()
        for j in range(1, chips):
            to_chip(j, x.at[chip], x.at[chip], sx_send.at[i, j - 1], sx_recv.at[i, chip]).wait_send()
        small_share(i, core).wait_send()
    for j in range(1, tensors):
        z_copy(j, lane).wait_send()


def store_kernel(count, *refs):
    sem = refs[-1]
    copies = [
        pltpu.make_async_copy(refs[i], refs[count + i], sem.at[i]) for i in range(count)
    ]
    for copy in copies:
        copy.start()
    for copy in copies:
        copy.wait()


def local(groups, tensors, kl, ka, ks, rl, ra, rs, gl, ga, gs, el, ea, es, eb, rate):
    chips = groups // 2
    f32 = jnp.float32
    rows, width = ka.shape[0] * ka.shape[1] // 2, ka.shape[2]
    chunks = 16
    while rows % (8 * chunks):
        chunks //= 2
    vocab, columns = ea.shape
    rank = eb.shape[1]
    padded = -(-vocab // 128) * 128
    blocks = columns // 128
    router_rows, experts = ra.shape
    gains, gain_rows = ga.shape
    operands = (
        rate.reshape(1),
        kl.reshape(2, rows, width), ka.reshape(2, rows, width), ks.reshape(2, rows, width),
        rl[0].T, ra.T, rs.T,
        gl[0], ga, gs,
        el.reshape(vocab, blocks, 128), ea, es, eb.T,
    )
    kv_shape, r_shape, g_shape, e_shape = (
        (2, rows, width), (experts, router_rows), (gains, gain_rows), (vocab, columns)
    )
    shapes = [s for s in (kv_shape, r_shape, g_shape, e_shape) for _ in range(3)]
    r_part, g_part, f_part = (
        (experts, router_rows // 2), (gains, gain_rows // 2), (rank // 2, padded)
    )
    vmem = lambda *s: pltpu.VMEM(s, f32)
    dma = lambda *s: pltpu.SemaphoreType.DMA(s)

    def sums(part, slots):
        return [vmem(2, *part), vmem(*part), vmem(chips, *part)] + slots + [vmem(2, *part)]

    scratch = [
        vmem(*kv_shape), vmem(*kv_shape), vmem(*kv_shape), vmem(rows, width), vmem(chips, rows, width),
        vmem(*r_shape), vmem(*r_shape), vmem(*r_shape),
        vmem(*g_shape), vmem(*g_shape), vmem(*g_shape),
        vmem(vocab, blocks, 128), vmem(*e_shape), vmem(*e_shape), vmem(rank, columns),
        vmem(padded, columns),
    ]
    scratch += sums(r_part, []) + sums(g_part, []) + sums(f_part, [vmem(tensors, *f_part)])
    peers = max(chips - 1, 1)
    scratch += [
        dma(2, chunks), dma(2, chunks), dma(2), dma(10),
        dma(chunks), dma(chunks), dma(peers, chunks), dma(chips, chunks), dma(chunks), dma(chunks),
        dma(3), dma(3), dma(3, peers), dma(3, chips), dma(3), dma(3),
        dma(max(tensors - 1, 1)), dma(tensors),
    ]
    hold = pl.pallas_call(
        functools.partial(exchange_kernel, chips, tensors, chunks, vocab),
        out_shape=[pltpu.VMEM(s, f32) for s in shapes],
        in_specs=[pl.BlockSpec(memory_space=pltpu.SMEM)] + [pl.BlockSpec(memory_space=pl.ANY)] * 13,
        out_specs=[pl.BlockSpec(memory_space=pltpu.VMEM)] * 12,
        scratch_shapes=scratch,
        compiler_params=pltpu.CompilerParams(
            collective_id=0, has_side_effects=True, vmem_limit_bytes=40 * 2**20
        ),
        name="exchange",
    )(*operands)
    out = pl.pallas_call(
        functools.partial(store_kernel, 12),
        out_shape=[jax.ShapeDtypeStruct(s, f32) for s in shapes],
        in_specs=[pl.BlockSpec(memory_space=pltpu.VMEM)] * 12,
        out_specs=[pl.BlockSpec(memory_space=pl.ANY)] * 12,
        scratch_shapes=[dma(12)],
        compiler_params=pltpu.CompilerParams(vmem_limit_bytes=20 * 2**20),
        name="store",
    )(*hold)
    return (
        *(o.reshape(ka.shape) for o in out[0:3]),
        *(o.T for o in out[3:6]),
        *out[6:9],
        *out[9:12],
    )


def solution(mesh):
    in_specs = (
        P("group", None, "dp", "tensor"),
        P(None, "dp", "tensor"),
        P(None, "dp", "tensor"),
        P("group", "dp", None),
        P("dp", None),
        P("dp", None),
        P("group", None, "dp"),
        P(None, "dp"),
        P(None, "dp"),
        P("group", "dp", "tensor"),
        P("dp", "tensor"),
        P("dp", "tensor"),
        P("tensor", None),
        P(),
    )
    out_specs = (
        P(None, "dp", "tensor"),
        P(None, "dp", "tensor"),
        P(None, "dp", "tensor"),
        P("dp", None),
        P("dp", None),
        P("dp", None),
        P(None, "dp"),
        P(None, "dp"),
        P(None, "dp"),
        P("dp", "tensor"),
        P("dp", "tensor"),
        P("dp", "tensor"),
    )
    body = functools.partial(local, mesh.shape["group"], mesh.shape["tensor"])
    return jax.shard_map(body, mesh=mesh, in_specs=in_specs, out_specs=out_specs, check_vma=False)
```

```python
import functools

import jax
import jax.numpy as jnp
from jax import lax
from jax.experimental import pallas as pl
from jax.experimental.pallas import tpu as pltpu
from jax.sharding import PartitionSpec as P

MESH = pl.DeviceIdType.MESH


def nesterov(average, state, anchor, rate):
    momentum = 0.5 * state + average
    return momentum, anchor - rate * (average + 0.5 * momentum)


def mean(total, groups):
    if groups & (groups - 1) == 0:
        return total * (1.0 / groups)
    return total / float(groups)


def exchange_kernel(
    chips, tensors, chunks, vocab,
    rate_ref, kl, ka, ks, rl, ra, rs, gl, ga, gs, el, ea, es, eb,
    k_avg, k_mom, k_upd, r_avg, r_mom, r_upd, g_avg, g_mom, g_upd, e_avg, e_mom, e_upd,
    a_v, l_v, s_v, pair_v, x_v,
    rl_v, ra_v, rs_v, gl_v, ga_v, gs_v, el_v, ea_v, es_v, eb_v, ed_v,
    r_d, r_pair, r_x, r_a, g_d, g_pair, g_x, g_a, f_d, f_pair, f_x, f_z, f_a,
    a_sem, l_sem, s_sem, small_sem,
    d_send, d_recv, x_send, x_recv, c_send, c_recv,
    sd_send, sd_recv, sx_send, sx_recv, sc_send, sc_recv, z_send, z_recv, go_sem, meet_sem,
):
    groups = 2 * chips
    me = lax.axis_index("group")
    chip, core = me // 2, lax.rem(me, 2)
    other = 1 - core
    sibling = chip * 2 + other
    lane = lax.axis_index("tensor")
    rows = a_v.shape[1] // chunks
    half_rows = a_v.shape[1]

    def load(src, dst, sem, half, c):
        at = pl.multiple_of(c * rows, rows)
        return pltpu.make_async_copy(
            src.at[half, pl.ds(at, rows), :], dst.at[half, pl.ds(at, rows), :], sem.at[half, c]
        )

    def start_loads(c, _):
        for half in (other, core):
            load(ka, a_v, a_sem, half, c).start()
            load(kl, l_v, l_sem, half, c).start()
        return 0

    small_loads = [
        pltpu.make_async_copy(src, dst, small_sem.at[i])
        for i, (src, dst) in enumerate(
            [(ea, ea_v), (el, el_v), (eb, eb_v), (rl, rl_v), (ra, ra_v), (gl, gl_v), (ga, ga_v),
             (rs, rs_v), (gs, gs_v), (es, es_v)]
        )
    ]
    lead = min(4, chunks)
    lax.fori_loop(0, lead, start_loads, 0)
    for copy in small_loads[:7]:
        copy.start()

    barrier = pltpu.get_barrier_semaphore()

    def greet(j):
        peer = lax.rem(chip + j, chips) * 2
        pl.semaphore_signal(barrier, inc=1, device_id={"group": peer}, device_id_type=MESH)

    for j in range(1, chips):
        greet(j)
    pl.when(core == 1)(lambda: greet(0))

    lax.fori_loop(lead, chunks, start_loads, 0)
    for copy in small_loads[7:]:
        copy.start()
    s_loads = [
        pltpu.make_async_copy(ks.at[half], s_v.at[half], s_sem.at[half]) for half in (0, 1)
    ]
    for copy in s_loads:
        copy.start()

    @pl.when(core == 0)
    def _():
        pl.semaphore_wait(barrier, groups - 1)
        pl.semaphore_signal(go_sem, inc=1, device_id={"group": sibling}, device_id_type=MESH)

    @pl.when(core == 1)
    def _():
        pl.semaphore_wait(go_sem, 1)
        for j in range(1, tensors):
            peer = lax.rem(lane + j, tensors)
            pl.semaphore_signal(barrier, inc=1, device_id={"tensor": peer}, device_id_type=MESH)

    def to_sibling(src, dst, send, recv):
        return pltpu.make_async_remote_copy(
            src_ref=src, dst_ref=dst, send_sem=send, recv_sem=recv,
            device_id={"group": sibling}, device_id_type=MESH,
        )

    def to_chip(j, src, dst, send, recv):
        return pltpu.make_async_remote_copy(
            src_ref=src, dst_ref=dst, send_sem=send, recv_sem=recv,
            device_id={"group": lax.rem(chip + j, chips) * 2 + core}, device_id_type=MESH,
        )

    def part(c):
        return pl.ds(pl.multiple_of(c * rows, rows), rows)

    def pair_copy(c):
        return to_sibling(l_v.at[other, part(c), :], pair_v.at[part(c), :], d_send.at[c], d_recv.at[c])

    def chip_copy(c, j, source):
        return to_chip(
            j, x_v.at[source, part(c), :], x_v.at[source, part(c), :],
            x_send.at[j - 1, c], x_recv.at[source, c],
        )

    def share_copy(c, half):
        return to_sibling(k_avg.at[half, part(c), :], k_avg.at[half, part(c), :], c_send.at[c], c_recv.at[c])

    def give(c):
        load(ka, a_v, a_sem, other, c).wait()
        load(kl, l_v, l_sem, other, c).wait()
        l_v[other, part(c), :] = a_v[other, part(c), :] - l_v[other, part(c), :]
        pair_copy(c).start()
        load(ka, a_v, a_sem, core, c).wait()
        load(kl, l_v, l_sem, core, c).wait()

    def send(c):
        copy = pair_copy(c)
        copy.wait_recv()
        x_v[chip, part(c), :] = (
            a_v[core, part(c), :] - l_v[core, part(c), :]
        ) + pair_v[part(c), :]
        for j in range(1, chips):
            chip_copy(c, j, chip).start()

    def give_and_send(c, _):
        give(c)
        send(c - 1)
        return 0

    give(0)
    lax.fori_loop(1, lead, give_and_send, 0)

    for copy in small_loads[:7]:
        copy.wait()
    smalls = [(r_d, r_pair, r_x, r_a), (g_d, g_pair, g_x, g_a), (f_d, f_pair, f_x, f_a)]

    ed_v[...] = jnp.zeros_like(ed_v)
    blocks = el_v.shape[1]
    for b in range(blocks):
        ed_v[0:vocab, b * 128 : (b + 1) * 128] = ea_v[:, b * 128 : (b + 1) * 128] - el_v[:, b, :]
    r_half = r_d.shape[2]
    g_half = g_d.shape[2]
    for h in (0, 1):
        r_d[h] = ra_v[:, h * r_half : (h + 1) * r_half] - rl_v[:, h * r_half : (h + 1) * r_half]
        g_d[h] = ga_v[:, h * g_half : (h + 1) * g_half] - gl_v[:, h * g_half : (h + 1) * g_half]
    factors = lax.dot_general(
        eb_v[...], ed_v[...], (((1,), (1,)), ((), ())),
        precision=lax.Precision.HIGHEST, preferred_element_type=jnp.float32,
    )
    rank_half = f_d.shape[1]
    for h in (0, 1):
        f_d[h] = factors[h * rank_half : (h + 1) * rank_half, :]
    small_pair = [
        to_sibling(d.at[other], pair, sd_send.at[i], sd_recv.at[i])
        for i, (d, pair, x, a) in enumerate(smalls)
    ]
    for copy in small_pair:
        copy.start()
    for i, (d, pair, x, a) in enumerate(smalls):
        small_pair[i].wait_recv()
        x[chip] = d[core] + pair[...]
        for j in range(1, chips):
            to_chip(j, x.at[chip], x.at[chip], sx_send.at[i, j - 1], sx_recv.at[i, chip]).start()

    lax.fori_loop(lead, chunks, give_and_send, 0)
    send(chunks - 1)
    for copy in s_loads + small_loads[7:]:
        copy.wait()

    rate = rate_ref[0]

    def gather(c):
        for j in range(1, chips):
            chip_copy(c, j, lax.rem(chip + j, chips)).wait_recv()
        total = x_v[0, part(c), :]
        for q in range(1, chips):
            total = total + x_v[q, part(c), :]
        average = mean(total, groups)
        k_avg[core, part(c), :] = average
        share_copy(c, core).start()
        momentum, updated = nesterov(average, s_v[core, part(c), :], a_v[core, part(c), :], rate)
        k_mom[core, part(c), :] = momentum
        k_upd[core, part(c), :] = updated

    def accept(c):
        share_copy(c, other).wait_recv()
        momentum, updated = nesterov(
            k_avg[other, part(c), :], s_v[other, part(c), :], a_v[other, part(c), :], rate
        )
        k_mom[other, part(c), :] = momentum
        k_upd[other, part(c), :] = updated

    def gather_and_accept(c, _):
        gather(c)
        accept(c - 1)
        return 0

    cut1 = max(lead, chunks // 2)
    cut2 = max(cut1, (3 * chunks) // 4)
    cut3 = max(cut2, (7 * chunks) // 8)
    gather(0)
    lax.fori_loop(1, cut1, gather_and_accept, 0)

    def small_share(i, half):
        a = smalls[i][3]
        return to_sibling(a.at[half], a.at[half], sc_send.at[i], sc_recv.at[i])

    def z_copy(j, source):
        return pltpu.make_async_remote_copy(
            src_ref=f_z.at[source], dst_ref=f_z.at[source], send_sem=z_send.at[j - 1],
            recv_sem=z_recv.at[source], device_id={"tensor": lax.rem(lane + j, tensors)},
            device_id_type=MESH,
        )

    @pl.when(core == 1)
    def _():
        pl.semaphore_wait(barrier, tensors - 1)
        pl.semaphore_signal(meet_sem, inc=1, device_id={"group": sibling}, device_id_type=MESH)

    @pl.when(core == 0)
    def _():
        pl.semaphore_wait(meet_sem, 1)

    for i, (d, pair, x, a) in enumerate(smalls):
        for j in range(1, chips):
            q = lax.rem(chip + j, chips)
            to_chip(j, x.at[q], x.at[q], sx_send.at[i, j - 1], sx_recv.at[i, q]).wait_recv()
        total = x[0]
        for q in range(1, chips):
            total = total + x[q]
        if i < 2:
            a[core] = mean(total, groups)
            small_share(i, core).start()
        else:
            f_z[lane] = total
            for j in range(1, tensors):
                z_copy(j, lane).start()

    lax.fori_loop(cut1, cut2, gather_and_accept, 0)

    for j in range(1, tensors):
        z_copy(j, lax.rem(lane + j, tensors)).wait_recv()
    total = f_z[0]
    for t in range(1, tensors):
        total = total + f_z[t]
    f_a[core] = mean(total, groups)
    small_share(2, core).start()
    for i, half, avg, mom, upd, a, st, an in (
        (0, r_half, r_avg, r_mom, r_upd, r_a, rs_v, ra_v),
        (1, g_half, g_avg, g_mom, g_upd, g_a, gs_v, ga_v),
    ):
        small_share(i, other).wait_recv()
        for h in (0, 1):
            at = slice(h * half, (h + 1) * half)
            average = a[h]
            momentum, updated = nesterov(average, st[:, at], an[:, at], rate)
            avg[:, at] = average
            mom[:, at] = momentum
            upd[:, at] = updated

    lax.fori_loop(cut2, cut3, gather_and_accept, 0)

    small_share(2, other).wait_recv()
    turned = jnp.concatenate([f_a[0], f_a[1]], axis=0).T
    average = lax.dot_general(
        turned, eb_v[...], (((1,), (0,)), ((), ())),
        precision=lax.Precision.HIGHEST, preferred_element_type=jnp.float32,
    )[0:vocab, :]
    momentum, updated = nesterov(average, es_v[...], ea_v[...], rate)
    e_avg[...] = average
    e_mom[...] = momentum
    e_upd[...] = updated

    lax.fori_loop(cut3, chunks, gather_and_accept, 0)
    accept(chunks - 1)

    def drain(c, _):
        pair_copy(c).wait_send()
        for j in range(1, chips):
            chip_copy(c, j, chip).wait_send()
        share_copy(c, core).wait_send()
        return 0

    lax.fori_loop(0, chunks, drain, 0)
    for i, (d, pair, x, a) in enumerate(smalls):
        small_pair[i].wait_send()
        for j in range(1, chips):
            to_chip(j, x.at[chip], x.at[chip], sx_send.at[i, j - 1], sx_recv.at[i, chip]).wait_send()
        small_share(i, core).wait_send()
    for j in range(1, tensors):
        z_copy(j, lane).wait_send()


def store_kernel(count, *refs):
    sem = refs[-1]
    copies = [
        pltpu.make_async_copy(refs[i], refs[count + i], sem.at[i]) for i in range(count)
    ]
    for copy in copies:
        copy.start()
    for copy in copies:
        copy.wait()


def local(groups, tensors, kl, ka, ks, rl, ra, rs, gl, ga, gs, el, ea, es, eb, rate):
    chips = groups // 2
    f32 = jnp.float32
    rows, width = ka.shape[0] * ka.shape[1] // 2, ka.shape[2]
    chunks = 16
    while rows % (8 * chunks):
        chunks //= 2
    vocab, columns = ea.shape
    rank = eb.shape[1]
    padded = -(-vocab // 128) * 128
    blocks = columns // 128
    router_rows, experts = ra.shape
    gains, gain_rows = ga.shape
    operands = (
        rate.reshape(1),
        kl.reshape(2, rows, width), ka.reshape(2, rows, width), ks.reshape(2, rows, width),
        rl[0].T, ra.T, rs.T,
        gl[0], ga, gs,
        el.reshape(vocab, blocks, 128), ea, es, eb.T,
    )
    kv_shape, r_shape, g_shape, e_shape = (
        (2, rows, width), (experts, router_rows), (gains, gain_rows), (vocab, columns)
    )
    shapes = [s for s in (kv_shape, r_shape, g_shape, e_shape) for _ in range(3)]
    r_part, g_part, f_part = (
        (experts, router_rows // 2), (gains, gain_rows // 2), (rank // 2, padded)
    )
    vmem = lambda *s: pltpu.VMEM(s, f32)
    dma = lambda *s: pltpu.SemaphoreType.DMA(s)

    def sums(part, slots):
        return [vmem(2, *part), vmem(*part), vmem(chips, *part)] + slots + [vmem(2, *part)]

    scratch = [
        vmem(*kv_shape), vmem(*kv_shape), vmem(*kv_shape), vmem(rows, width), vmem(chips, rows, width),
        vmem(*r_shape), vmem(*r_shape), vmem(*r_shape),
        vmem(*g_shape), vmem(*g_shape), vmem(*g_shape),
        vmem(vocab, blocks, 128), vmem(*e_shape), vmem(*e_shape), vmem(rank, columns),
        vmem(padded, columns),
    ]
    scratch += sums(r_part, []) + sums(g_part, []) + sums(f_part, [vmem(tensors, *f_part)])
    peers = max(chips - 1, 1)
    scratch += [
        dma(2, chunks), dma(2, chunks), dma(2), dma(10),
        dma(chunks), dma(chunks), dma(peers, chunks), dma(chips, chunks), dma(chunks), dma(chunks),
        dma(3), dma(3), dma(3, peers), dma(3, chips), dma(3), dma(3),
        dma(max(tensors - 1, 1)), dma(tensors),
        pltpu.SemaphoreType.REGULAR, pltpu.SemaphoreType.REGULAR,
    ]
    hold = pl.pallas_call(
        functools.partial(exchange_kernel, chips, tensors, chunks, vocab),
        out_shape=[pltpu.VMEM(s, f32) for s in shapes],
        in_specs=[pl.BlockSpec(memory_space=pltpu.SMEM)] + [pl.BlockSpec(memory_space=pltpu.HBM)] * 13,
        out_specs=[pl.BlockSpec(memory_space=pltpu.VMEM)] * 12,
        scratch_shapes=scratch,
        compiler_params=pltpu.CompilerParams(
            collective_id=0, has_side_effects=True, vmem_limit_bytes=40 * 2**20
        ),
        name="exchange",
    )(*[pltpu.with_memory_space_constraint(o, pltpu.HBM) if o.ndim > 1 else o for o in operands])
    out = pl.pallas_call(
        functools.partial(store_kernel, 12),
        out_shape=[jax.ShapeDtypeStruct(s, f32) for s in shapes],
        in_specs=[pl.BlockSpec(memory_space=pltpu.VMEM)] * 12,
        out_specs=[pl.BlockSpec(memory_space=pltpu.HBM)] * 12,
        scratch_shapes=[dma(12)],
        compiler_params=pltpu.CompilerParams(vmem_limit_bytes=20 * 2**20),
        name="store",
    )(*hold)
    return (
        *(o.reshape(ka.shape) for o in out[0:3]),
        *(o.T for o in out[3:6]),
        *out[6:9],
        *out[9:12],
    )


def solution(mesh):
    in_specs = (
        P("group", None, "dp", "tensor"),
        P(None, "dp", "tensor"),
        P(None, "dp", "tensor"),
        P("group", "dp", None),
        P("dp", None),
        P("dp", None),
        P("group", None, "dp"),
        P(None, "dp"),
        P(None, "dp"),
        P("group", "dp", "tensor"),
        P("dp", "tensor"),
        P("dp", "tensor"),
        P("tensor", None),
        P(),
    )
    out_specs = (
        P(None, "dp", "tensor"),
        P(None, "dp", "tensor"),
        P(None, "dp", "tensor"),
        P("dp", None),
        P("dp", None),
        P("dp", None),
        P(None, "dp"),
        P(None, "dp"),
        P(None, "dp"),
        P("dp", "tensor"),
        P("dp", "tensor"),
        P("dp", "tensor"),
    )
    body = functools.partial(local, mesh.shape["group"], mesh.shape["tensor"])
    return jax.shard_map(body, mesh=mesh, in_specs=in_specs, out_specs=out_specs, check_vma=False)
```

```python
import functools

import jax
import jax.numpy as jnp
from jax import lax
from jax.experimental import pallas as pl
from jax.experimental.pallas import tpu as pltpu
from jax.sharding import PartitionSpec as P

MESH = pl.DeviceIdType.MESH
SIZES = (1, 3, 5, 8, 8, 5, 2)


def nesterov(average, state, anchor, rate):
    momentum = 0.5 * state + average
    return momentum, anchor - rate * (average + 0.5 * momentum)


def mean(total, groups):
    if groups & (groups - 1) == 0:
        return total * (1.0 / groups)
    return total / float(groups)


def exchange_kernel(
    chips, tensors, sizes, vocab,
    rate_ref, kl, ka, ks, rl, ra, rs, gl, ga, gs, el, ea, es, eb,
    k_avg, k_mom, k_upd, r_avg, r_mom, r_upd, g_avg, g_mom, g_upd, e_avg, e_mom, e_upd,
    a_v, l_v, s_v, pair_v, x_v,
    rl_v, ra_v, rs_v, gl_v, ga_v, gs_v, el_v, ea_v, es_v, eb_v, ed_v,
    r_d, r_pair, r_x, r_a, g_d, g_pair, g_x, g_a, f_d, f_pair, f_x, f_z, f_a,
    a_sem, l_sem, s_sem, small_sem,
    d_send, d_recv, x_send, x_recv, c_send, c_recv,
    sd_send, sd_recv, sx_send, sx_recv, sc_send, sc_recv, z_send, z_recv, go_sem, meet_sem,
):
    groups = 2 * chips
    me = lax.axis_index("group")
    chip, core = me // 2, lax.rem(me, 2)
    other = 1 - core
    sibling = chip * 2 + other
    lane = lax.axis_index("tensor")
    chunks = len(sizes)
    starts = [sum(sizes[:c]) for c in range(chunks)]

    def load(src, dst, sem, half, c):
        return pltpu.make_async_copy(
            src.at[half, part(c), :], dst.at[half, part(c), :], sem.at[half, c]
        )

    def part(c):
        return pl.ds(starts[c], sizes[c])

    def start_loads(c):
        for half in (other, core):
            load(ka, a_v, a_sem, half, c).start()
            load(kl, l_v, l_sem, half, c).start()

    small_loads = [
        pltpu.make_async_copy(src, dst, small_sem.at[i])
        for i, (src, dst) in enumerate(
            [(ea, ea_v), (el, el_v), (eb, eb_v), (rl, rl_v), (ra, ra_v), (gl, gl_v), (ga, ga_v),
             (rs, rs_v), (gs, gs_v), (es, es_v)]
        )
    ]
    lead = min(3, chunks)
    for c in range(lead):
        start_loads(c)
    for copy in small_loads[:7]:
        copy.start()

    barrier = pltpu.get_barrier_semaphore()

    def greet(j):
        peer = lax.rem(chip + j, chips) * 2
        pl.semaphore_signal(barrier, inc=1, device_id={"group": peer}, device_id_type=MESH)

    for j in range(1, chips):
        greet(j)
    pl.when(core == 1)(lambda: greet(0))

    for c in range(lead, chunks):
        start_loads(c)
    for copy in small_loads[7:]:
        copy.start()
    s_loads = [
        pltpu.make_async_copy(ks.at[half], s_v.at[half], s_sem.at[half]) for half in (0, 1)
    ]
    for copy in s_loads:
        copy.start()

    @pl.when(core == 0)
    def _():
        pl.semaphore_wait(barrier, groups - 1)
        pl.semaphore_signal(go_sem, inc=1, device_id={"group": sibling}, device_id_type=MESH)

    @pl.when(core == 1)
    def _():
        pl.semaphore_wait(go_sem, 1)
        for j in range(1, tensors):
            peer = lax.rem(lane + j, tensors)
            pl.semaphore_signal(barrier, inc=1, device_id={"tensor": peer}, device_id_type=MESH)

    def to_sibling(src, dst, send, recv):
        return pltpu.make_async_remote_copy(
            src_ref=src, dst_ref=dst, send_sem=send, recv_sem=recv,
            device_id={"group": sibling}, device_id_type=MESH,
        )

    def to_chip(j, src, dst, send, recv):
        return pltpu.make_async_remote_copy(
            src_ref=src, dst_ref=dst, send_sem=send, recv_sem=recv,
            device_id={"group": lax.rem(chip + j, chips) * 2 + core}, device_id_type=MESH,
        )

    def pair_copy(c):
        return to_sibling(l_v.at[other, part(c), :], pair_v.at[part(c), :], d_send.at[c], d_recv.at[c])

    def chip_copy(c, j, source):
        return to_chip(
            j, x_v.at[source, part(c), :], x_v.at[source, part(c), :],
            x_send.at[j - 1, c], x_recv.at[source, c],
        )

    def share_copy(c, half):
        return to_sibling(k_avg.at[half, part(c), :], k_avg.at[half, part(c), :], c_send.at[c], c_recv.at[c])

    def give(c):
        load(ka, a_v, a_sem, other, c).wait()
        load(kl, l_v, l_sem, other, c).wait()
        l_v[other, part(c), :] = a_v[other, part(c), :] - l_v[other, part(c), :]
        pair_copy(c).start()
        load(ka, a_v, a_sem, core, c).wait()
        load(kl, l_v, l_sem, core, c).wait()

    def send(c):
        copy = pair_copy(c)
        copy.wait_recv()
        x_v[chip, part(c), :] = (
            a_v[core, part(c), :] - l_v[core, part(c), :]
        ) + pair_v[part(c), :]
        for j in range(1, chips):
            chip_copy(c, j, chip).start()

    def give_and_send(first, last):
        for c in range(first, last):
            give(c)
            send(c - 1)

    give(0)
    give_and_send(1, lead)

    for copy in small_loads[:7]:
        copy.wait()
    smalls = [(r_d, r_pair, r_x, r_a), (g_d, g_pair, g_x, g_a), (f_d, f_pair, f_x, f_a)]

    ed_v[...] = jnp.zeros_like(ed_v)
    blocks = el_v.shape[1]
    for b in range(blocks):
        ed_v[0:vocab, b * 128 : (b + 1) * 128] = ea_v[:, b * 128 : (b + 1) * 128] - el_v[:, b, :]
    r_half = r_d.shape[2]
    g_half = g_d.shape[2]
    for h in (0, 1):
        r_d[h] = ra_v[:, h * r_half : (h + 1) * r_half] - rl_v[:, h * r_half : (h + 1) * r_half]
        g_d[h] = ga_v[:, h * g_half : (h + 1) * g_half] - gl_v[:, h * g_half : (h + 1) * g_half]
    factors = lax.dot_general(
        eb_v[...], ed_v[...], (((1,), (1,)), ((), ())),
        precision=lax.Precision.HIGHEST, preferred_element_type=jnp.float32,
    )
    rank_half = f_d.shape[1]
    for h in (0, 1):
        f_d[h] = factors[h * rank_half : (h + 1) * rank_half, :]
    small_pair = [
        to_sibling(d.at[other], pair, sd_send.at[i], sd_recv.at[i])
        for i, (d, pair, x, a) in enumerate(smalls)
    ]
    for copy in small_pair:
        copy.start()
    for i, (d, pair, x, a) in enumerate(smalls):
        small_pair[i].wait_recv()
        x[chip] = d[core] + pair[...]
        for j in range(1, chips):
            to_chip(j, x.at[chip], x.at[chip], sx_send.at[i, j - 1], sx_recv.at[i, chip]).start()

    give_and_send(lead, chunks)
    send(chunks - 1)
    for copy in s_loads + small_loads[7:]:
        copy.wait()

    rate = rate_ref[0]

    def gather(c):
        for j in range(1, chips):
            chip_copy(c, j, lax.rem(chip + j, chips)).wait_recv()
        total = x_v[0, part(c), :]
        for q in range(1, chips):
            total = total + x_v[q, part(c), :]
        average = mean(total, groups)
        k_avg[core, part(c), :] = average
        share_copy(c, core).start()
        momentum, updated = nesterov(average, s_v[core, part(c), :], a_v[core, part(c), :], rate)
        k_mom[core, part(c), :] = momentum
        k_upd[core, part(c), :] = updated

    def accept(c):
        share_copy(c, other).wait_recv()
        momentum, updated = nesterov(
            k_avg[other, part(c), :], s_v[other, part(c), :], a_v[other, part(c), :], rate
        )
        k_mom[other, part(c), :] = momentum
        k_upd[other, part(c), :] = updated

    def gather_and_accept(first, last):
        for c in range(first, last):
            gather(c)
            accept(c - 1)

    cut1, cut2, cut3 = (min(lead + k, chunks) for k in (1, 2, 3))
    gather(0)
    gather_and_accept(1, cut1)

    def small_share(i, half):
        a = smalls[i][3]
        return to_sibling(a.at[half], a.at[half], sc_send.at[i], sc_recv.at[i])

    def z_copy(j, source):
        return pltpu.make_async_remote_copy(
            src_ref=f_z.at[source], dst_ref=f_z.at[source], send_sem=z_send.at[j - 1],
            recv_sem=z_recv.at[source], device_id={"tensor": lax.rem(lane + j, tensors)},
            device_id_type=MESH,
        )

    @pl.when(core == 1)
    def _():
        pl.semaphore_wait(barrier, tensors - 1)
        pl.semaphore_signal(meet_sem, inc=1, device_id={"group": sibling}, device_id_type=MESH)

    @pl.when(core == 0)
    def _():
        pl.semaphore_wait(meet_sem, 1)

    for i, (d, pair, x, a) in enumerate(smalls):
        for j in range(1, chips):
            q = lax.rem(chip + j, chips)
            to_chip(j, x.at[q], x.at[q], sx_send.at[i, j - 1], sx_recv.at[i, q]).wait_recv()
        total = x[0]
        for q in range(1, chips):
            total = total + x[q]
        if i < 2:
            a[core] = mean(total, groups)
            small_share(i, core).start()
        else:
            f_z[lane] = total
            for j in range(1, tensors):
                z_copy(j, lane).start()

    gather_and_accept(cut1, cut2)

    for j in range(1, tensors):
        z_copy(j, lax.rem(lane + j, tensors)).wait_recv()
    total = f_z[0]
    for t in range(1, tensors):
        total = total + f_z[t]
    f_a[core] = mean(total, groups)
    small_share(2, core).start()
    for i, half, avg, mom, upd, a, st, an in (
        (0, r_half, r_avg, r_mom, r_upd, r_a, rs_v, ra_v),
        (1, g_half, g_avg, g_mom, g_upd, g_a, gs_v, ga_v),
    ):
        small_share(i, other).wait_recv()
        for h in (0, 1):
            at = slice(h * half, (h + 1) * half)
            average = a[h]
            momentum, updated = nesterov(average, st[:, at], an[:, at], rate)
            avg[:, at] = average
            mom[:, at] = momentum
            upd[:, at] = updated

    gather_and_accept(cut2, cut3)

    small_share(2, other).wait_recv()
    turned = jnp.concatenate([f_a[0], f_a[1]], axis=0).T
    average = lax.dot_general(
        turned, eb_v[...], (((1,), (0,)), ((), ())),
        precision=lax.Precision.HIGHEST, preferred_element_type=jnp.float32,
    )[0:vocab, :]
    momentum, updated = nesterov(average, es_v[...], ea_v[...], rate)
    e_avg[...] = average
    e_mom[...] = momentum
    e_upd[...] = updated

    gather_and_accept(cut3, chunks)
    accept(chunks - 1)

    for c in range(chunks):
        pair_copy(c).wait_send()
        for j in range(1, chips):
            chip_copy(c, j, chip).wait_send()
        share_copy(c, core).wait_send()
    for i, (d, pair, x, a) in enumerate(smalls):
        small_pair[i].wait_send()
        for j in range(1, chips):
            to_chip(j, x.at[chip], x.at[chip], sx_send.at[i, j - 1], sx_recv.at[i, chip]).wait_send()
        small_share(i, core).wait_send()
    for j in range(1, tensors):
        z_copy(j, lane).wait_send()


def store_kernel(count, *refs):
    sem = refs[-1]
    copies = [
        pltpu.make_async_copy(refs[i], refs[count + i], sem.at[i]) for i in range(count)
    ]
    for copy in copies:
        copy.start()
    for copy in copies:
        copy.wait()


def local(groups, tensors, kl, ka, ks, rl, ra, rs, gl, ga, gs, el, ea, es, eb, rate):
    chips = groups // 2
    f32 = jnp.float32
    rows, width = ka.shape[0] * ka.shape[1] // 2, ka.shape[2]
    sizes = tuple(k * rows // 32 for k in SIZES) if rows % 256 == 0 else (rows,)
    chunks = len(sizes)
    vocab, columns = ea.shape
    rank = eb.shape[1]
    padded = -(-vocab // 128) * 128
    blocks = columns // 128
    router_rows, experts = ra.shape
    gains, gain_rows = ga.shape
    operands = (
        rate.reshape(1),
        kl.reshape(2, rows, width), ka.reshape(2, rows, width), ks.reshape(2, rows, width),
        rl[0].T, ra.T, rs.T,
        gl[0], ga, gs,
        el.reshape(vocab, blocks, 128), ea, es, eb.T,
    )
    kv_shape, r_shape, g_shape, e_shape = (
        (2, rows, width), (experts, router_rows), (gains, gain_rows), (vocab, columns)
    )
    shapes = [s for s in (kv_shape, r_shape, g_shape, e_shape) for _ in range(3)]
    r_part, g_part, f_part = (
        (experts, router_rows // 2), (gains, gain_rows // 2), (rank // 2, padded)
    )
    vmem = lambda *s: pltpu.VMEM(s, f32)
    dma = lambda *s: pltpu.SemaphoreType.DMA(s)

    def sums(part, slots):
        return [vmem(2, *part), vmem(*part), vmem(chips, *part)] + slots + [vmem(2, *part)]

    scratch = [
        vmem(*kv_shape), vmem(*kv_shape), vmem(*kv_shape), vmem(rows, width), vmem(chips, rows, width),
        vmem(*r_shape), vmem(*r_shape), vmem(*r_shape),
        vmem(*g_shape), vmem(*g_shape), vmem(*g_shape),
        vmem(vocab, blocks, 128), vmem(*e_shape), vmem(*e_shape), vmem(rank, columns),
        vmem(padded, columns),
    ]
    scratch += sums(r_part, []) + sums(g_part, []) + sums(f_part, [vmem(tensors, *f_part)])
    peers = max(chips - 1, 1)
    scratch += [
        dma(2, chunks), dma(2, chunks), dma(2), dma(10),
        dma(chunks), dma(chunks), dma(peers, chunks), dma(chips, chunks), dma(chunks), dma(chunks),
        dma(3), dma(3), dma(3, peers), dma(3, chips), dma(3), dma(3),
        dma(max(tensors - 1, 1)), dma(tensors),
        pltpu.SemaphoreType.REGULAR, pltpu.SemaphoreType.REGULAR,
    ]
    hold = pl.pallas_call(
        functools.partial(exchange_kernel, chips, tensors, sizes, vocab),
        out_shape=[pltpu.VMEM(s, f32) for s in shapes],
        in_specs=[pl.BlockSpec(memory_space=pltpu.SMEM)] + [pl.BlockSpec(memory_space=pltpu.HBM)] * 13,
        out_specs=[pl.BlockSpec(memory_space=pltpu.VMEM)] * 12,
        scratch_shapes=scratch,
        compiler_params=pltpu.CompilerParams(
            collective_id=0, has_side_effects=True, vmem_limit_bytes=40 * 2**20
        ),
        name="exchange",
    )(*[pltpu.with_memory_space_constraint(o, pltpu.HBM) if o.ndim > 1 else o for o in operands])
    out = pl.pallas_call(
        functools.partial(store_kernel, 12),
        out_shape=[jax.ShapeDtypeStruct(s, f32) for s in shapes],
        in_specs=[pl.BlockSpec(memory_space=pltpu.VMEM)] * 12,
        out_specs=[pl.BlockSpec(memory_space=pltpu.HBM)] * 12,
        scratch_shapes=[dma(12)],
        compiler_params=pltpu.CompilerParams(vmem_limit_bytes=20 * 2**20),
        name="store",
    )(*hold)
    return (
        *(o.reshape(ka.shape) for o in out[0:3]),
        *(o.T for o in out[3:6]),
        *out[6:9],
        *out[9:12],
    )


def solution(mesh):
    in_specs = (
        P("group", None, "dp", "tensor"),
        P(None, "dp", "tensor"),
        P(None, "dp", "tensor"),
        P("group", "dp", None),
        P("dp", None),
        P("dp", None),
        P("group", None, "dp"),
        P(None, "dp"),
        P(None, "dp"),
        P("group", "dp", "tensor"),
        P("dp", "tensor"),
        P("dp", "tensor"),
        P("tensor", None),
        P(),
    )
    out_specs = (
        P(None, "dp", "tensor"),
        P(None, "dp", "tensor"),
        P(None, "dp", "tensor"),
        P("dp", None),
        P("dp", None),
        P("dp", None),
        P(None, "dp"),
        P(None, "dp"),
        P(None, "dp"),
        P("dp", "tensor"),
        P("dp", "tensor"),
        P("dp", "tensor"),
    )
    body = functools.partial(local, mesh.shape["group"], mesh.shape["tensor"])
    return jax.shard_map(body, mesh=mesh, in_specs=in_specs, out_specs=out_specs, check_vma=False)
```
